256 devices in a mesh: vir: 64 (over x_lo, z, y), occ: 4 (over x_hi, core).
Axes of the slice: x: 4 (x_hi: 2, x_lo: 2; x = x_hi * 2 + x_lo), y: 4, z: 8, core: 2. Of those that a mesh axis runs over, the one named last changes fastest.
Arguments:
- cholesky_c: bfloat16 [2560, 1024, 16], P('vir'), may hold values from -0.75 to 0.75
- cholesky_d: bfloat16 [2560, 1024, 16], P('vir'), may hold values from -0.75 to 0.75
- amplitudes: bfloat16 [512, 256], P('occ'), may hold values from -0.375 to 0.375
Outputs:
- residual: bfloat16 [512, 256, 4096], P('occ', 'vir')
The draws below stay inside these ranges and needn't reach their ends.
All inputs are finite; a program needn't handle non-finite values.
Results may differ from the reference program's by a relative error of at most 0.0049.
Values may be sent and summed in bfloat16 or wider, within the bound.
A program may use at most 192 MiB of HBM per device.

```python
import jax
import jax.numpy as jnp
from jax import lax

V = 1024
Q = 2560
CT = 16
AH = 64
BH = 64
IJ = 512


def level_of(rng, dims, cuts, low, top_value):
    loudness = 1.0
    for dim, shards_of in cuts:
        steps = jax.random.uniform(jax.random.fold_in(jax.random.fold_in(rng, 6), dim), (shards_of,), jnp.float32, low / len(cuts), top_value / len(cuts))
        loudness = loudness * jnp.repeat(jnp.exp(steps), dims[dim] // shards_of).reshape((-1,) + (1,) * (len(dims) - 1 - dim))
    return loudness


def noise(key, shape, deviation, bound, cuts=(), held_as=jnp.bfloat16):
    level = level_of(key, shape, cuts, -0.22, 0.18) if cuts else 1.0
    entries = jax.random.normal(key, shape, jnp.float32) * deviation * level
    return jnp.minimum(jnp.maximum(entries, -bound), bound).astype(held_as)


def setup_inputs(seed: int = 0) -> dict:
    keys = jax.random.split(jax.random.key(seed), 4)
    return {
        "cholesky_c": noise(keys[0], (Q, V, CT), 0.125, 0.75, ((0, 64),)),
        "cholesky_d": noise(keys[1], (Q, V, CT), 0.125, 0.75, ((0, 64),)),
        "amplitudes": noise(keys[2], (IJ, CT * CT), (CT * CT) ** -0.5, 0.375, ((0, 4),)),
    }


def reference(cholesky_c, cholesky_d, amplitudes):
    row_blocks = V // AH
    col_blocks = V // BH
    stacked = cholesky_c.reshape(Q, row_blocks, AH, CT)
    amp_wide = amplitudes.astype(jnp.float32)
    right_vectors = cholesky_d.astype(jnp.float32)

    def one_row(row_index, output):
        start = row_index.astype(jnp.int32)
        block_c = lax.dynamic_index_in_dim(stacked, start, 1, keepdims=False).astype(jnp.float32)
        integrals = jnp.einsum("qac,qbd->abcd", block_c, right_vectors).astype(jnp.bfloat16)
        integrals = lax.optimization_barrier(integrals)
        integrals = integrals.reshape(AH, col_blocks, BH, CT * CT).astype(jnp.float32)
        contracted = jnp.einsum("ix,akbx->ikab", amp_wide, integrals).astype(jnp.bfloat16)
        contracted = contracted.reshape(IJ, 1, col_blocks * AH * BH)
        return lax.dynamic_update_slice_in_dim(output, contracted, start, 1)

    output = jnp.zeros((IJ, row_blocks, col_blocks * AH * BH), jnp.bfloat16)
    output = lax.fori_loop(0, row_blocks, one_row, output)
    return output.reshape(IJ, row_blocks * col_blocks, AH * BH)
```

```python
import functools

import jax
import jax.numpy as jnp
from jax import lax
from jax.experimental import pallas as pl
from jax.experimental.pallas import tpu as pltpu
from jax.sharding import PartitionSpec as P

MESH = pl.DeviceIdType.MESH
F32 = jnp.float32
BF16 = jnp.bfloat16

NX, NY, NZ, NK = 4, 4, 8, 2
OFFSETS = (0, -1, 1, -2, 2, -3, 3, 4)
FROM_BELOW = ((-1, 0), (-1, 1), (-2, 0), (-2, 1), (-3, 0), (-3, 1), (4, 0))
FROM_ABOVE = ((1, 1), (1, 0), (2, 1), (2, 0), (3, 1), (3, 0), (4, 1))
GROUPS = ((0, 2), (2, 4), (6, 4), (10, 4), (14, 2))


def slot_of(offset, other):
    return 2 * OFFSETS.index(offset) + other


def place():
    v, o = lax.axis_index("vir"), lax.axis_index("occ")
    x = (o // NK) * 2 + v // (NZ * NY)
    return x, v % NY, (v // NY) % NZ, o % NK


def device(x, y, z, k):
    x, y, z, k = (x + NX) % NX, (y + NY) % NY, (z + NZ) % NZ, (k + NK) % NK
    return ((x % 2) * NZ + z) * NY + y, (x // 2) * NK + k


def kernel(
    c_ref, d_ref, amp_ref, out_ref,
    c_slab, c_send, c_raw, d_raw, rows, c_full, d_full, acc, spread, ints, amps, result,
    load_sem, amp_sems, c1_send, c1_recv, c2_send, c2_recv, c3_send, c3_recv, dy_send, dy_recv,
    z_send, z_recv, x_send, x_recv, out_sem, outs_send, outs_recv,
):
    x, y, z, k = place()
    side = 1 - 2 * k
    low = lax.broadcasted_iota(jnp.int32, (16, 128), 1) < 64

    barrier = pltpu.get_barrier_semaphore()
    greeted = []
    for offset in OFFSETS:
        if offset:
            greeted.append(device(x, y, z + offset, k))
        greeted.append(device(x - side, y, z + offset, k))
    greeted.append(device(x + side, y, z, k))
    greeted += [device(x, y + step, z, k) for step in (1, 2, 3)]
    greeted.append(device(x, y, z, k + 1))
    for target in greeted:
        pl.semaphore_signal(barrier, inc=1, device_id=target, device_id_type=MESH)

    load = pltpu.make_async_copy(c_ref.at[k], c_slab, load_sem.at[0])
    load.start()
    own_d = pltpu.make_async_copy(
        d_ref.at[:, :, :, pl.ds(pl.multiple_of(256 * y + 128 * k, 128), 128)], d_raw.at[:, y], load_sem.at[1]
    )
    own_d.start()
    load.wait()

    def pair_up(p, _):
        for m in range(8):
            first = c_slab[2 * p, :, 128 * m : 128 * (m + 1)].astype(F32)
            second = c_slab[2 * p + 1, :, 128 * m : 128 * (m + 1)].astype(F32)
            c_send[2 * m, p] = jnp.where(low, first, pltpu.roll(second, 64, 1)).astype(BF16)
            c_send[2 * m + 1, p] = jnp.where(low, pltpu.roll(first, 64, 1), second).astype(BF16)
        return 0

    lax.fori_loop(0, 10, pair_up, 0)
    amps[k] = amp_ref[...]

    pl.semaphore_wait(barrier, len(greeted))

    dy = []
    for step in (1, 2, 3):
        to = (y + step) % NY
        copy = pltpu.make_async_remote_copy(
            src_ref=d_ref.at[:, :, :, pl.ds(pl.multiple_of(256 * to + 128 * k, 128), 128)],
            dst_ref=d_raw.at[:, y],
            send_sem=dy_send.at[step - 1], recv_sem=dy_recv.at[step - 1],
            device_id=device(x, to, z, k), device_id_type=MESH,
        )
        copy.start()
        dy.append(copy)

    c1 = {}
    for offset in OFFSETS:
        for other in (0, 1):
            slot = slot_of(offset, other)
            to_x = (x + other * side + NX) % NX
            to_z = (z - offset + NZ) % NZ
            piece = c_send.at[(to_x % 2) * NZ + to_z]
            if slot == 0:
                copy = pltpu.make_async_copy(piece, c_raw.at[0, y], load_sem.at[0])
            else:
                copy = pltpu.make_async_remote_copy(
                    src_ref=piece, dst_ref=c_raw.at[slot, y],
                    send_sem=c1_send.at[slot], recv_sem=c1_recv.at[slot],
                    device_id=device(to_x, y, to_z, k), device_id_type=MESH,
                )
            copy.start()
            c1[slot] = copy
    amp_copy = pltpu.make_async_remote_copy(
        src_ref=amps.at[k], dst_ref=amps.at[k], send_sem=amp_sems.at[0], recv_sem=amp_sems.at[1],
        device_id=device(x, y, z, k + 1), device_id_type=MESH,
    )
    amp_copy.start()

    c2 = {}

    def c_forward(group):
        start, count = GROUPS[group]
        for slot in range(start, start + count):
            if slot == 0:
                c1[slot].wait()
            else:
                c1[slot].wait_recv()
        mine = c_raw.at[pl.ds(start, count), y]
        for step in (1, 3, 2):
            copy = pltpu.make_async_remote_copy(
                src_ref=mine, dst_ref=mine,
                send_sem=c2_send.at[group, step - 1], recv_sem=c2_recv.at[group, step - 1],
                device_id=device(x, y + step, z, k), device_id_type=MESH,
            )
            copy.start()
            c2[group, step] = copy

    c3 = {}

    def c_rows(group):
        start, count = GROUPS[group]
        for step in (1, 2, 3):
            c2[group, step].wait_recv()

        def one_slot(slot, _):
            rows[0:640, :] = c_raw[slot].reshape(640, 128).astype(F32)
            lower = lax.broadcasted_iota(jnp.int32, (40, 128), 1) < 64
            for m in range(8):
                first = rows[pl.ds(2 * m, 40, stride=16), :]
                second = rows[pl.ds(2 * m + 1, 40, stride=16), :]
                both = jnp.concatenate(
                    [
                        jnp.where(lower, first, pltpu.roll(second, 64, 1)),
                        jnp.where(lower, pltpu.roll(first, 64, 1), second),
                    ],
                    axis=0,
                )
                c_full[slot, k, :, 128 * m : 128 * (m + 1)] = both.astype(BF16)
            return 0

        lax.fori_loop(start, start + count, one_slot, 0)
        half = c_full.at[pl.ds(start, count), k]
        c3[group] = pltpu.make_async_remote_copy(
            src_ref=half, dst_ref=half, send_sem=c3_send.at[group], recv_sem=c3_recv.at[group],
            device_id=device(x, y, z, k + 1), device_id_type=MESH,
        )
        c3[group].start()

    sent = []

    def x_copy(h, offset, half):
        copy = pltpu.make_async_remote_copy(
            src_ref=d_full.at[h, slot_of(offset, 0), half],
            dst_ref=d_full.at[h, slot_of(offset, 1), half],
            send_sem=x_send.at[h, half, OFFSETS.index(offset)],
            recv_sem=x_recv.at[h, half, OFFSETS.index(offset)],
            device_id=device(x + 1 - 2 * half, y, z, k), device_id_type=MESH,
        )
        return copy

    def x_start(h, offset, half):
        copy = x_copy(h, offset, half)
        copy.start()
        sent.append(copy)

    def z_copy(h, way, i):
        offset, half = (FROM_BELOW, FROM_ABOVE)[way][i]
        before = (offset + 1 if way == 0 else offset - 1) if offset != 4 else (-3 if way == 0 else 3)
        return pltpu.make_async_remote_copy(
            src_ref=d_full.at[h, slot_of(before, 0), half],
            dst_ref=d_full.at[h, slot_of(offset, 0), half],
            send_sem=z_send.at[h, way, i], recv_sem=z_recv.at[h, way, i],
            device_id=device(x, y, z + 1 - 2 * way, k), device_id_type=MESH,
        )

    def z_start(h, way, i):
        copy = z_copy(h, way, i)
        copy.start()
        sent.append(copy)

    def own_start(h):
        for i in (0, 1):
            for way in (0, 1):
                z_start(h, way, i)
        for half in (0, 1):
            x_start(h, 0, half)

    def step(h, i):
        for way in (0, 1):
            z_copy(h, way, i).wait_recv()
            if i + 2 < 7:
                z_start(h, way, i + 2)
            x_start(h, *(FROM_BELOW, FROM_ABOVE)[way][i])

    def await_x(h, group):
        start, count = GROUPS[group]
        for slot in range(start, start + count, 2):
            for half in (0, 1):
                x_copy(h, OFFSETS[slot // 2], half).wait_recv()

    def multiply(h, group):
        start, count = GROUPS[group]
        last = group == len(GROUPS) - 1

        def one_tile(m, _):
            columns = pl.ds(pl.multiple_of(256 * m, 256), 256)
            left = c_full[start : start + count, :, :, columns].reshape(160 * count, 256)
            right = d_full[h, start : start + count].reshape(160 * count, 1024)
            term = lax.dot_general(left, right, (((0,), (0,)), ((), ())), preferred_element_type=F32)
            if group:
                term += acc[columns, :]
            if not last:
                acc[columns, :] = term
            else:
                for c in range(4):
                    for d in range(8):
                        spread[d, pl.ds(4 * m + c, 64, stride=16), :] = term[
                            64 * c : 64 * (c + 1), 128 * d : 128 * (d + 1)
                        ]
            return 0

        lax.fori_loop(0, 4, one_tile, 0)

    def round_off(h):
        def one_pair(pair, _):
            for d in range(8):
                for odd in (0, 1):
                    at = pl.multiple_of(32 * pair + 16 * odd, 16)
                    ints[pair, 16 * (8 * h + d) : 16 * (8 * h + d + 1), 128 * odd : 128 * (odd + 1)] = (
                        spread[d, pl.ds(at, 16), :].astype(BF16)
                    )
            return 0

        lax.fori_loop(0, 32, one_pair, 0)

    c_forward(0)

    own_d.wait()
    for copy in dy:
        copy.wait_recv()

    def d_rows(half, _):
        rows[...] = d_raw[half].reshape(1280, 128).astype(F32)
        for h in range(2):
            for d in range(8):
                both = jnp.concatenate(
                    [rows[pl.ds(16 * odd + 8 * h + d, 40, stride=32), :] for odd in (0, 1)], axis=0
                )
                d_full[h, 0, half, :, 128 * d : 128 * (d + 1)] = both.astype(BF16)
        return 0

    lax.fori_loop(0, 2, d_rows, 0)
    own_start(0)
    c_forward(1)
    step(0, 0)
    c_forward(2)
    c_rows(0)
    step(0, 1)
    c_forward(3)
    c_rows(1)
    step(0, 2)
    c_forward(4)
    c3[0].wait_recv()
    await_x(0, 0)
    multiply(0, 0)
    step(0, 3)
    c_rows(2)
    step(0, 4)
    c3[1].wait_recv()
    await_x(0, 1)
    multiply(0, 1)
    own_start(1)
    step(0, 5)
    c_rows(3)
    step(0, 6)
    c3[2].wait_recv()
    await_x(0, 2)
    multiply(0, 2)
    step(1, 0)
    c_rows(4)
    c3[3].wait_recv()
    await_x(0, 3)
    multiply(0, 3)
    step(1, 1)
    c3[4].wait_recv()
    await_x(0, 4)
    multiply(0, 4)
    step(1, 2)
    round_off(0)
    await_x(1, 0)
    multiply(1, 0)
    step(1, 3)
    await_x(1, 1)
    multiply(1, 1)
    step(1, 4)
    step(1, 5)
    await_x(1, 2)
    multiply(1, 2)
    step(1, 6)
    await_x(1, 3)
    multiply(1, 3)
    amp_copy.wait_recv()
    await_x(1, 4)
    multiply(1, 4)
    round_off(1)

    lower = lax.broadcasted_iota(jnp.int32, (256, 128), 1) < 64
    finals = []
    for part in range(4):

        def one_pair(pair, _):
            total = jnp.dot(amps[...].reshape(256, 256), ints[pair], preferred_element_type=F32)
            first, second = total[:, :128], total[:, 128:]
            columns = pl.ds(pl.multiple_of(128 * pair, 128), 128)
            result[0, :, columns] = jnp.where(lower, first, pltpu.roll(second, 64, 1)).astype(BF16)
            result[1, :, columns] = jnp.where(lower, pltpu.roll(first, 64, 1), second).astype(BF16)
            return 0

        lax.fori_loop(8 * part, 8 * (part + 1), one_pair, 0)
        columns = pl.ds(1024 * part, 1024)
        into = out_ref.at[pl.ds(2 * k, 2), :, columns]
        mine = pltpu.make_async_copy(
            result.at[:, pl.ds(pl.multiple_of(128 * k, 128), 128), columns], into, out_sem.at[part]
        )
        theirs = pltpu.make_async_remote_copy(
            src_ref=result.at[:, pl.ds(pl.multiple_of(128 - 128 * k, 128), 128), columns], dst_ref=into,
            send_sem=outs_send.at[part], recv_sem=outs_recv.at[part],
            device_id=device(x, y, z, k + 1), device_id_type=MESH,
        )
        theirs.start()
        mine.start()
        finals += [mine, theirs]

    for copy in dy + [c1[slot] for slot in range(1, 16)] + list(c2.values()) + list(c3.values()) + [amp_copy] + sent:
        copy.wait_send()
    for copy in finals:
        copy.wait()


def body(cholesky_c, cholesky_d, amplitudes):
    slab_c = jnp.transpose(cholesky_c, (0, 2, 1)).reshape(2, 20, 16, 1024)
    slab_d = jnp.transpose(cholesky_d, (0, 2, 1)).reshape(2, 20, 16, 1024)
    amps = jnp.transpose(amplitudes.reshape(128, 16, 16), (0, 2, 1)).reshape(128, 256)
    dma = pltpu.SemaphoreType.DMA
    out = pl.pallas_call(
        kernel,
        out_shape=jax.ShapeDtypeStruct((4, 128, 4096), BF16),
        in_specs=[
            pl.BlockSpec(memory_space=pl.ANY),
            pl.BlockSpec(memory_space=pl.ANY),
            pl.BlockSpec(memory_space=pltpu.VMEM),
        ],
        out_specs=pl.BlockSpec(memory_space=pl.ANY),
        scratch_shapes=[
            pltpu.VMEM((20, 16, 1024), BF16),
            pltpu.VMEM((16, 10, 16, 128), BF16),
            pltpu.VMEM((16, 4, 10, 16, 128), BF16),
            pltpu.VMEM((2, 4, 20, 16, 128), BF16),
            pltpu.VMEM((1280, 128), F32),
            pltpu.VMEM((16, 2, 80, 1024), BF16),
            pltpu.VMEM((2, 16, 2, 80, 1024), BF16),
            pltpu.VMEM((1024, 1024), F32),
            pltpu.VMEM((8, 1024, 128), F32),
            pltpu.VMEM((32, 256, 256), BF16),
            pltpu.VMEM((2, 128, 256), BF16),
            pltpu.VMEM((2, 256, 4096), BF16),
            dma((2,)), dma((2,)), dma((16,)), dma((16,)), dma((5, 3)), dma((5, 3)), dma((5,)), dma((5,)),
            dma((3,)), dma((3,)), dma((2, 2, 7)), dma((2, 2, 7)), dma((2, 2, 8)), dma((2, 2, 8)),
            dma((4,)), dma((4,)), dma((4,)),
        ],
        compiler_params=pltpu.CompilerParams(
            collective_id=0, has_side_effects=True, vmem_limit_bytes=56 * 2**20
        ),
        cost_estimate=pl.CostEstimate(flops=13_000_000_000, bytes_accessed=8_000_000, transcendentals=0),
    )(slab_c, slab_d, amps)
    return jnp.transpose(out, (1, 0, 2))


def solution(mesh):
    return jax.shard_map(
        body,
        mesh=mesh,
        in_specs=(P("vir", None, None), P("vir", None, None), P("occ", None)),
        out_specs=P("occ", "vir", None),
        check_vma=False,
    )
```

```python
import functools

import jax
import jax.numpy as jnp
from jax import lax
from jax.experimental import pallas as pl
from jax.experimental.pallas import tpu as pltpu
from jax.sharding import PartitionSpec as P

MESH = pl.DeviceIdType.MESH
F32 = jnp.float32
BF16 = jnp.bfloat16

NX, NY, NZ, NK = 4, 4, 8, 2
OFFSETS = (0, -1, 1, -2, 2, -3, 3, 4)
PARTS = ((0, 0), (0, 1), (1, 0), (1, 1))
ARRIVALS = tuple(
    tuple((sign * hops, h, half) for hops in (1, 2, 3) for h, half in PARTS) + ((4, 0, way), (4, 1, way))
    for way, sign in ((0, -1), (1, 1))
)
SPANS = ((0, 8), (8, 16))
GROUPS = ((0, 2), (2, 4), (6, 4), (10, 4), (14, 2))


def slot_of(offset, other):
    return 2 * OFFSETS.index(offset) + other


def place():
    v, o = lax.axis_index("vir"), lax.axis_index("occ")
    x = (o // NK) * 2 + v // (NZ * NY)
    return x, v % NY, (v // NY) % NZ, o % NK


def device(x, y, z, k):
    x, y, z, k = (x + NX) % NX, (y + NY) % NY, (z + NZ) % NZ, (k + NK) % NK
    return ((x % 2) * NZ + z) * NY + y, (x // 2) * NK + k


def kernel(
    c_ref, d_ref, amp_ref, out_ref,
    c_slab, c_send, c_in, c_raw, d_raw, rows, c_full, d_first, d_second, acc, spread, ints, amps, result,
    load_sem, amp_sems, c1_send, c1_recv, cx_send, cx_recv, c2_send, c2_recv, c3_send, c3_recv, dy_send, dy_recv,
    z_send, z_recv, x_send, x_recv, out_sem, outs_send, outs_recv,
):
    x, y, z, k = place()
    x_low, share = x % 2, 5 * (x // 2)
    d_full = (d_first, d_second)
    low = lax.broadcasted_iota(jnp.int32, (16, 128), 1) < 64

    barrier = pltpu.get_barrier_semaphore()
    greeted = []
    greeted += [device(x, y, z + offset, k) for offset in OFFSETS if offset]
    greeted += [device(x + step, y, z, k) for step in (1, 3)]
    greeted += [device(x, y + step, z, k) for step in (1, 2, 3)]
    greeted.append(device(x, y, z, k + 1))
    for target in greeted:
        pl.semaphore_signal(barrier, inc=1, device_id=target, device_id_type=MESH)

    load = pltpu.make_async_copy(c_ref.at[k], c_slab, load_sem.at[0])
    load.start()
    own_d = pltpu.make_async_copy(
        d_ref.at[:, :, :, pl.ds(pl.multiple_of(256 * y + 128 * k, 128), 128)], d_raw.at[:, y], load_sem.at[1]
    )
    own_d.start()
    pl.semaphore_wait(barrier, len(greeted))

    def columns_of(to, half):
        return d_ref.at[half, :, :, pl.ds(pl.multiple_of(256 * to + 128 * k, 128), 128)]

    dy = {}
    for half in (0, 1):
        for step in (1, 3, 2):
            to = (y + step) % NY
            copy = pltpu.make_async_remote_copy(
                src_ref=columns_of(to, half), dst_ref=d_raw.at[half, y],
                send_sem=dy_send.at[half, step - 1], recv_sem=dy_recv.at[half, step - 1],
                device_id=device(x, to, z, k), device_id_type=MESH,
            )
            copy.start()
            dy[half, step] = copy
    load.wait()

    def pair_up(p, _):
        for m in range(8):
            first = c_slab[2 * p, :, 128 * m : 128 * (m + 1)].astype(F32)
            second = c_slab[2 * p + 1, :, 128 * m : 128 * (m + 1)].astype(F32)
            c_send[m // 4, 2 * m % 8, p] = jnp.where(low, first, pltpu.roll(second, 64, 1)).astype(BF16)
            c_send[m // 4, 2 * m % 8 + 1, p] = jnp.where(low, pltpu.roll(first, 64, 1), second).astype(BF16)
        return 0

    lax.fori_loop(0, 10, pair_up, 0)
    c1, c1_other = {}, {}
    for offset in OFFSETS[1:]:
        to_z = (z - offset + NZ) % NZ
        index = OFFSETS.index(offset)
        for other, copies in ((1, c1_other), (0, c1)):
            copies[offset] = pltpu.make_async_remote_copy(
                src_ref=c_send.at[1 - x_low, to_z, pl.ds(share, 5)] if other else c_send.at[x_low, to_z],
                dst_ref=c_in.at[index] if other else c_raw.at[slot_of(offset, 0), y],
                send_sem=c1_send.at[other, index], recv_sem=c1_recv.at[other, index],
                device_id=device(x, y, to_z, k), device_id_type=MESH,
            )
            copies[offset].start()
    own_c = pltpu.make_async_copy(c_send.at[x_low, z], c_raw.at[0, y], load_sem.at[0])
    own_c.start()

    old, new = (lax.broadcasted_iota(jnp.int32, (256, 256), axis) for axis in (0, 1))
    swap = (old == (new % 16) * 16 + new // 16).astype(F32).astype(BF16)
    amps[k] = jnp.dot(amp_ref[...], swap, preferred_element_type=F32).astype(BF16)
    amp_copy = pltpu.make_async_remote_copy(
        src_ref=amps.at[k], dst_ref=amps.at[k], send_sem=amp_sems.at[0], recv_sem=amp_sems.at[1],
        device_id=device(x, y, z, k + 1), device_id_type=MESH,
    )
    amp_copy.start()

    cx = {}

    def c_across(offset):
        index = OFFSETS.index(offset)
        if offset:
            c1_other[offset].wait_recv()
        for step in (1, 3):
            cx[offset, step] = pltpu.make_async_remote_copy(
                src_ref=c_in.at[index] if offset else c_send.at[1 - x_low, z, pl.ds(share, 5)],
                dst_ref=c_raw.at[slot_of(offset, 1), y, pl.ds(share, 5)],
                send_sem=cx_send.at[index, step // 2], recv_sem=cx_recv.at[index, step // 2],
                device_id=device(x + step, y, z, k), device_id_type=MESH,
            )
            cx[offset, step].start()

    c2 = {}

    def c_forward(group):
        start, count = GROUPS[group]
        for offset in OFFSETS[start // 2 : (start + count) // 2]:
            if offset:
                c1[offset].wait_recv()
            else:
                own_c.wait()
            for step in (1, 3):
                cx[offset, step].wait_recv()
        mine = c_raw.at[pl.ds(start, count), y]
        for step in (1, 3, 2):
            copy = pltpu.make_async_remote_copy(
                src_ref=mine, dst_ref=mine,
                send_sem=c2_send.at[group, step - 1], recv_sem=c2_recv.at[group, step - 1],
                device_id=device(x, y + step, z, k), device_id_type=MESH,
            )
            copy.start()
            c2[group, step] = copy

    c3 = {}

    def c_rows(group):
        start, count = GROUPS[group]
        for step in (1, 2, 3):
            c2[group, step].wait_recv()

        def one_slot(slot, _):
            rows[0:640, :] = c_raw[slot].reshape(640, 128).astype(F32)
            lower = lax.broadcasted_iota(jnp.int32, (40, 128), 1) < 64
            for m in range(8):
                first = rows[pl.ds(2 * m, 40, stride=16), :]
                second = rows[pl.ds(2 * m + 1, 40, stride=16), :]
                both = jnp.concatenate(
                    [
                        jnp.where(lower, first, pltpu.roll(second, 64, 1)),
                        jnp.where(lower, pltpu.roll(first, 64, 1), second),
                    ],
                    axis=0,
                )
                c_full[slot, k, :, 128 * m : 128 * (m + 1)] = both.astype(BF16)
            return 0

        lax.fori_loop(start, start + count, one_slot, 0)
        half = c_full.at[pl.ds(start, count), k]
        c3[group] = pltpu.make_async_remote_copy(
            src_ref=half, dst_ref=half, send_sem=c3_send.at[group], recv_sem=c3_recv.at[group],
            device_id=device(x, y, z, k + 1), device_id_type=MESH,
        )
        c3[group].start()

    sent = []

    def x_copy(h, offset, half):
        copy = pltpu.make_async_remote_copy(
            src_ref=d_full[h].at[slot_of(offset, 0), half],
            dst_ref=d_full[h].at[slot_of(offset, 1), half],
            send_sem=x_send.at[h, half, OFFSETS.index(offset)],
            recv_sem=x_recv.at[h, half, OFFSETS.index(offset)],
            device_id=device(x + 1 - 2 * (half if offset else h), y, z, k), device_id_type=MESH,
        )
        return copy

    def x_start(h, offset, half):
        copy = x_copy(h, offset, half)
        copy.start()
        sent.append(copy)

    def z_copy(way, i):
        offset, h, half = ARRIVALS[way][i]
        before = (offset + 1 if way == 0 else offset - 1) if offset != 4 else (-3 if way == 0 else 3)
        return pltpu.make_async_remote_copy(
            src_ref=d_full[h].at[slot_of(before, 0), half],
            dst_ref=d_full[h].at[slot_of(offset, 0), half],
            send_sem=z_send.at[way, i], recv_sem=z_recv.at[way, i],
            device_id=device(x, y, z + 1 - 2 * way, k), device_id_type=MESH,
        )

    def z_start(way, i):
        copy = z_copy(way, i)
        copy.start()
        sent.append(copy)

    def own_start(h, half):
        for way in (0, 1):
            z_start(way, PARTS.index((h, half)))

    def step(i):
        for way in (0, 1):
            z_copy(way, i).wait_recv()
            offset, h, half = ARRIVALS[way][i]
            after = offset - 1 if way == 0 else offset + 1
            onward = (4 if after == -4 else after, h, half)
            if onward in ARRIVALS[way]:
                z_start(way, ARRIVALS[way].index(onward))
            x_start(h, offset, half)

    def await_x(h, group):
        start, count = GROUPS[group]
        for slot in range(start, start + count, 2):
            for half in (0, 1):
                x_copy(h, OFFSETS[slot // 2], half).wait_recv()

    def multiply(h, group):
        start, count = GROUPS[group]
        last = group == len(GROUPS) - 1
        values = SPANS[h][1] - SPANS[h][0]

        def one_tile(m, _):
            columns = pl.ds(pl.multiple_of(256 * m, 256), 256)
            left = c_full[start : start + count, :, :, columns].reshape(160 * count, 256)
            right = d_full[h][start : start + count].reshape(160 * count, 128 * values)
            term = lax.dot_general(left, right, (((0,), (0,)), ((), ())), preferred_element_type=F32)
            if group:
                term += acc[columns, 128 * SPANS[h][0] : 128 * SPANS[h][1]]
            if not last:
                acc[columns, 128 * SPANS[h][0] : 128 * SPANS[h][1]] = term
            else:
                for c in range(4):
                    for d in range(values):
                        spread[d, pl.ds(4 * m + c, 64, stride=16), :] = term[
                            64 * c : 64 * (c + 1), 128 * d : 128 * (d + 1)
                        ]
            return 0

        lax.fori_loop(0, 4, one_tile, 0, unroll=4 if last else 2)

    def term(h, group):
        if not h:
            c3[group].wait_recv()
        await_x(h, group)
        multiply(h, group)

    def round_off(h):
        start, stop = SPANS[h]

        def one_pair(pair, _):
            for d in range(start, stop):
                first = spread[d - start, pl.ds(pl.multiple_of(32 * pair, 16), 16), :]
                second = spread[d - start, pl.ds(pl.multiple_of(32 * pair + 16, 16), 16), :]
                at = slice(16 * d, 16 * (d + 1))
                ints[pair, at, 0:128] = jnp.where(low, first, pltpu.roll(second, 64, 1)).astype(BF16)
                ints[pair, at, 128:256] = jnp.where(low, pltpu.roll(first, 64, 1), second).astype(BF16)
            return 0

        lax.fori_loop(0, 32, one_pair, 0, unroll=8)

    c_across(0)

    def d_rows(half):
        rows[...] = d_raw[half].reshape(1280, 128).astype(F32)
        for h, (start, stop) in enumerate(SPANS):
            for d in range(start, stop):
                both = jnp.concatenate([rows[pl.ds(16 * odd + d, 40, stride=32), :] for odd in (0, 1)], axis=0)
                d_full[h][0, half, :, 128 * (d - start) : 128 * (d - start + 1)] = both.astype(BF16)

    own_d.wait()
    for half in (0, 1):
        for step_y in (1, 3, 2):
            dy[half, step_y].wait_recv()
        d_rows(half)
        own_start(0, half)
        x_start(0, 0, half)
        x_start(1, 0, half)
    own_start(1, 0)
    own_start(1, 1)
    for offset in OFFSETS[1:]:
        c_across(offset)
    c_forward(0)
    c_forward(1)
    step(0)
    c_forward(2)
    step(1)
    c_forward(3)
    c_forward(4)
    c_rows(0)
    step(2)
    step(3)
    c_rows(1)
    term(0, 0)
    step(4)
    term(1, 0)
    step(5)
    c_rows(2)
    term(0, 1)
    step(6)
    term(1, 1)
    step(7)
    step(8)
    c_rows(3)
    term(0, 2)
    step(9)
    c_rows(4)
    term(1, 2)
    step(10)
    step(11)
    step(12)
    term(0, 3)
    step(13)
    term(1, 3)
    amp_copy.wait_recv()
    term(0, 4)
    round_off(0)
    term(1, 4)
    round_off(1)

    finals = []
    for part in range(4):

        def one_pair(pair, _):
            total = jnp.dot(amps[...].reshape(256, 256), ints[pair], preferred_element_type=F32)
            columns = pl.ds(pl.multiple_of(128 * pair, 128), 128)
            result[0, :, columns] = total[:, :128].astype(BF16)
            result[1, :, columns] = total[:, 128:].astype(BF16)
            return 0

        lax.fori_loop(8 * part, 8 * (part + 1), one_pair, 0, unroll=8)
        columns = pl.ds(1024 * part, 1024)
        into = out_ref.at[pl.ds(2 * k, 2), :, columns]
        mine = pltpu.make_async_copy(
            result.at[:, pl.ds(pl.multiple_of(128 * k, 128), 128), columns], into, out_sem.at[part]
        )
        theirs = pltpu.make_async_remote_copy(
            src_ref=result.at[:, pl.ds(pl.multiple_of(128 - 128 * k, 128), 128), columns], dst_ref=into,
            send_sem=outs_send.at[part], recv_sem=outs_recv.at[part],
            device_id=device(x, y, z, k + 1), device_id_type=MESH,
        )
        theirs.start()
        mine.start()
        finals += [mine, theirs]

    for copy in list(dy.values()) + list(c1.values()) + list(c1_other.values()) + list(cx.values()) + list(c2.values()) + list(c3.values()) + [amp_copy] + sent:
        copy.wait_send()
    for copy in finals:
        copy.wait()


def blocks_inward(in_ref, out_ref):
    out_ref[...] = jnp.swapaxes(in_ref[...], 0, 1)


def body(cholesky_c, cholesky_d, amplitudes):
    slab_c = jnp.transpose(cholesky_c, (0, 2, 1)).reshape(2, 20, 16, 1024)
    slab_d = jnp.transpose(cholesky_d, (0, 2, 1)).reshape(2, 20, 16, 1024)
    dma = pltpu.SemaphoreType.DMA
    out = pl.pallas_call(
        kernel,
        out_shape=jax.ShapeDtypeStruct((4, 128, 4096), BF16),
        in_specs=[
            pl.BlockSpec(memory_space=pl.ANY),
            pl.BlockSpec(memory_space=pl.ANY),
            pl.BlockSpec(memory_space=pltpu.VMEM),
        ],
        out_specs=pl.BlockSpec(memory_space=pl.ANY),
        scratch_shapes=[
            pltpu.VMEM((20, 16, 1024), BF16),
            pltpu.VMEM((2, 8, 10, 16, 128), BF16),
            pltpu.VMEM((8, 5, 16, 128), BF16),
            pltpu.VMEM((16, 4, 10, 16, 128), BF16),
            pltpu.VMEM((2, 4, 20, 16, 128), BF16),
            pltpu.VMEM((1280, 128), F32),
            pltpu.VMEM((16, 2, 80, 1024), BF16),
            *(pltpu.VMEM((16, 2, 80, 128 * (stop - start)), BF16) for start, stop in SPANS),
            pltpu.VMEM((1024, 2048), F32),
            pltpu.VMEM((SPANS[0][1], 1024, 128), F32),
            pltpu.VMEM((32, 256, 256), BF16),
            pltpu.VMEM((2, 128, 256), BF16),
            pltpu.VMEM((2, 256, 4096), BF16),
            dma((2,)), dma((2,)), dma((2, 8)), dma((2, 8)), dma((8, 2)), dma((8, 2)), dma((5, 3)), dma((5, 3)), dma((5,)), dma((5,)),
            dma((2, 3)), dma((2, 3)), dma((2, 14)), dma((2, 14)), dma((2, 2, 8)), dma((2, 2, 8)),
            dma((4,)), dma((4,)), dma((4,)),
        ],
        compiler_params=pltpu.CompilerParams(
            collective_id=0, has_side_effects=True, vmem_limit_bytes=63 * 2**20
        ),
        cost_estimate=pl.CostEstimate(flops=13_000_000_000, bytes_accessed=8_000_000, transcendentals=0),
    )(slab_c, slab_d, amplitudes)
    return pl.pallas_call(
        blocks_inward,
        grid=(2,),
        out_shape=jax.ShapeDtypeStruct((128, 4, 4096), BF16),
        in_specs=[pl.BlockSpec((4, 128, 2048), lambda i: (0, 0, i))],
        out_specs=pl.BlockSpec((128, 4, 2048), lambda i: (0, 0, i)),
        compiler_params=pltpu.CompilerParams(vmem_limit_bytes=56 * 2**20),
    )(out)


def solution(mesh):
    return jax.shard_map(
        body,
        mesh=mesh,
        in_specs=(P("vir", None, None), P("vir", None, None), P("occ", None)),
        out_specs=P("occ", "vir", None),
        check_vma=False,
    )
```

```python
import functools

import jax
import jax.numpy as jnp
from jax import lax
from jax.experimental import pallas as pl
from jax.experimental.pallas import tpu as pltpu
from jax.sharding import PartitionSpec as P

MESH = pl.DeviceIdType.MESH
F32 = jnp.float32
BF16 = jnp.bfloat16

NX, NY, NZ, NK = 4, 4, 8, 2
OFFSETS = (0, -1, 1, -2, 2, -3, 3, 4)
PARTS = ((0, 0), (0, 1), (1, 0), (1, 1))
ARRIVALS = tuple(
    tuple((sign * hops, h, half) for hops in (1, 2, 3) for h, half in PARTS) + ((4, 0, way), (4, 1, way))
    for way, sign in ((0, -1), (1, 1))
)
SPANS = ((0, 8), (8, 16))
GROUPS = ((0, 2), (2, 4), (6, 4), (10, 4), (14, 2))


def slot_of(offset, other):
    return 2 * OFFSETS.index(offset) + other


def place():
    v, o = lax.axis_index("vir"), lax.axis_index("occ")
    x = (o // NK) * 2 + v // (NZ * NY)
    return x, v % NY, (v // NY) % NZ, o % NK


def device(x, y, z, k):
    x, y, z, k = (x + NX) % NX, (y + NY) % NY, (z + NZ) % NZ, (k + NK) % NK
    return ((x % 2) * NZ + z) * NY + y, (x // 2) * NK + k


def kernel(
    c_ref, d_ref, amp_ref, out_ref,
    c_slab, c_send, c_in, c_raw, d_raw, rows, c_full, d_first, d_second, acc, spread, ints, amps, result,
    load_sem, amp_sems, c1_send, c1_recv, cx_send, cx_recv, c2_send, c2_recv, c3_send, c3_recv, dy_send, dy_recv,
    z_send, z_recv, x_send, x_recv, outs_send, outs_recv,
):
    x, y, z, k = place()
    x_low, share = x % 2, 5 * (x // 2)
    d_full = (d_first, d_second)
    low = lax.broadcasted_iota(jnp.int32, (16, 128), 1) < 64

    barrier = pltpu.get_barrier_semaphore()
    greeted = []
    greeted += [device(x, y, z + offset, k) for offset in OFFSETS if offset]
    greeted += [device(x + step, y, z, k) for step in (1, 3)]
    greeted += [device(x, y + step, z, k) for step in (1, 2, 3)]
    greeted.append(device(x, y, z, k + 1))
    for target in greeted:
        pl.semaphore_signal(barrier, inc=1, device_id=target, device_id_type=MESH)

    load = pltpu.make_async_copy(c_ref.at[k], c_slab, load_sem.at[0])
    load.start()
    own_d = pltpu.make_async_copy(
        d_ref.at[:, :, :, pl.ds(pl.multiple_of(256 * y + 128 * k, 128), 128)], d_raw.at[:, y], load_sem.at[1]
    )
    own_d.start()
    pl.semaphore_wait(barrier, len(greeted))

    def columns_of(to, half):
        return d_ref.at[half, :, :, pl.ds(pl.multiple_of(256 * to + 128 * k, 128), 128)]

    dy = {}
    for half in (0, 1):
        for step in (1, 3, 2):
            to = (y + step) % NY
            copy = pltpu.make_async_remote_copy(
                src_ref=columns_of(to, half), dst_ref=d_raw.at[half, y],
                send_sem=dy_send.at[half, step - 1], recv_sem=dy_recv.at[half, step - 1],
                device_id=device(x, to, z, k), device_id_type=MESH,
            )
            copy.start()
            dy[half, step] = copy
    load.wait()

    def pair_up(p, _):
        for m in range(8):
            first = c_slab[2 * p, :, 128 * m : 128 * (m + 1)].astype(F32)
            second = c_slab[2 * p + 1, :, 128 * m : 128 * (m + 1)].astype(F32)
            c_send[m // 4, 2 * m % 8, p] = jnp.where(low, first, pltpu.roll(second, 64, 1)).astype(BF16)
            c_send[m // 4, 2 * m % 8 + 1, p] = jnp.where(low, pltpu.roll(first, 64, 1), second).astype(BF16)
        return 0

    lax.fori_loop(0, 10, pair_up, 0)
    c1, c1_other = {}, {}
    for offset in OFFSETS[1:]:
        to_z = (z - offset + NZ) % NZ
        index = OFFSETS.index(offset)
        for other, copies in ((1, c1_other), (0, c1)):
            copies[offset] = pltpu.make_async_remote_copy(
                src_ref=c_send.at[1 - x_low, to_z, pl.ds(share, 5)] if other else c_send.at[x_low, to_z],
                dst_ref=c_in.at[index] if other else c_raw.at[slot_of(offset, 0), y],
                send_sem=c1_send.at[other, index], recv_sem=c1_recv.at[other, index],
                device_id=device(x, y, to_z, k), device_id_type=MESH,
            )
            copies[offset].start()
    own_c = pltpu.make_async_copy(c_send.at[x_low, z], c_raw.at[0, y], load_sem.at[0])
    own_c.start()

    old, new = (lax.broadcasted_iota(jnp.int32, (256, 256), axis) for axis in (0, 1))
    swap = (old == (new % 16) * 16 + new // 16).astype(F32).astype(BF16)
    amps[0] = jnp.dot(amp_ref[...], swap, preferred_element_type=F32).astype(BF16)
    amp_copy = pltpu.make_async_remote_copy(
        src_ref=amps.at[0], dst_ref=amps.at[1], send_sem=amp_sems.at[0], recv_sem=amp_sems.at[1],
        device_id=device(x, y, z, k + 1), device_id_type=MESH,
    )
    amp_copy.start()

    cx = {}

    def c_across(offset):
        index = OFFSETS.index(offset)
        if offset:
            c1_other[offset].wait_recv()
        for step in (1, 3):
            cx[offset, step] = pltpu.make_async_remote_copy(
                src_ref=c_in.at[index] if offset else c_send.at[1 - x_low, z, pl.ds(share, 5)],
                dst_ref=c_raw.at[slot_of(offset, 1), y, pl.ds(share, 5)],
                send_sem=cx_send.at[index, step // 2], recv_sem=cx_recv.at[index, step // 2],
                device_id=device(x + step, y, z, k), device_id_type=MESH,
            )
            cx[offset, step].start()

    c2 = {}

    def c_forward(group):
        start, count = GROUPS[group]
        for offset in OFFSETS[start // 2 : (start + count) // 2]:
            if offset:
                c1[offset].wait_recv()
            else:
                own_c.wait()
            for step in (1, 3):
                cx[offset, step].wait_recv()
        mine = c_raw.at[pl.ds(start, count), y]
        for step in (1, 3, 2):
            copy = pltpu.make_async_remote_copy(
                src_ref=mine, dst_ref=mine,
                send_sem=c2_send.at[group, step - 1], recv_sem=c2_recv.at[group, step - 1],
                device_id=device(x, y + step, z, k), device_id_type=MESH,
            )
            copy.start()
            c2[group, step] = copy

    c3 = {}

    def c_rows(group):
        start, count = GROUPS[group]
        for step in (1, 2, 3):
            c2[group, step].wait_recv()

        def one_slot(slot, _):
            rows[0:640, :] = c_raw[slot].reshape(640, 128).astype(F32)
            lower = lax.broadcasted_iota(jnp.int32, (40, 128), 1) < 64
            for m in range(8):
                first = rows[pl.ds(2 * m, 40, stride=16), :]
                second = rows[pl.ds(2 * m + 1, 40, stride=16), :]
                both = jnp.concatenate(
                    [
                        jnp.where(lower, first, pltpu.roll(second, 64, 1)),
                        jnp.where(lower, pltpu.roll(first, 64, 1), second),
                    ],
                    axis=0,
                )
                c_full[slot, k, :, 128 * m : 128 * (m + 1)] = both.astype(BF16)
            return 0

        lax.fori_loop(start, start + count, one_slot, 0)
        half = c_full.at[pl.ds(start, count), k]
        c3[group] = pltpu.make_async_remote_copy(
            src_ref=half, dst_ref=half, send_sem=c3_send.at[group], recv_sem=c3_recv.at[group],
            device_id=device(x, y, z, k + 1), device_id_type=MESH,
        )
        c3[group].start()

    sent = []

    def x_copy(h, offset, half):
        copy = pltpu.make_async_remote_copy(
            src_ref=d_full[h].at[slot_of(offset, 0), half],
            dst_ref=d_full[h].at[slot_of(offset, 1), half],
            send_sem=x_send.at[h, half, OFFSETS.index(offset)],
            recv_sem=x_recv.at[h, half, OFFSETS.index(offset)],
            device_id=device(x + 1 - 2 * (half if offset else h), y, z, k), device_id_type=MESH,
        )
        return copy

    def x_start(h, offset, half):
        copy = x_copy(h, offset, half)
        copy.start()
        sent.append(copy)

    def z_copy(way, i):
        offset, h, half = ARRIVALS[way][i]
        before = (offset + 1 if way == 0 else offset - 1) if offset != 4 else (-3 if way == 0 else 3)
        return pltpu.make_async_remote_copy(
            src_ref=d_full[h].at[slot_of(before, 0), half],
            dst_ref=d_full[h].at[slot_of(offset, 0), half],
            send_sem=z_send.at[way, i], recv_sem=z_recv.at[way, i],
            device_id=device(x, y, z + 1 - 2 * way, k), device_id_type=MESH,
        )

    def z_start(way, i):
        copy = z_copy(way, i)
        copy.start()
        sent.append(copy)

    def own_start(h, half):
        for way in (0, 1):
            z_start(way, PARTS.index((h, half)))

    def step(i):
        for way in (0, 1):
            z_copy(way, i).wait_recv()
            offset, h, half = ARRIVALS[way][i]
            after = offset - 1 if way == 0 else offset + 1
            onward = (4 if after == -4 else after, h, half)
            if onward in ARRIVALS[way]:
                z_start(way, ARRIVALS[way].index(onward))
            x_start(h, offset, half)

    def await_x(h, group):
        start, count = GROUPS[group]
        for slot in range(start, start + count, 2):
            for half in (0, 1):
                x_copy(h, OFFSETS[slot // 2], half).wait_recv()

    def multiply(h, group):
        start, count = GROUPS[group]
        last = group == len(GROUPS) - 1
        values = SPANS[h][1] - SPANS[h][0]

        def one_tile(m, _):
            columns = pl.ds(pl.multiple_of(256 * m, 256), 256)
            left = c_full[start : start + count, :, :, columns].reshape(160 * count, 256)
            right = d_full[h][start : start + count].reshape(160 * count, 128 * values)
            term = lax.dot_general(left, right, (((0,), (0,)), ((), ())), preferred_element_type=F32)
            if group:
                term += acc[columns, 128 * SPANS[h][0] : 128 * SPANS[h][1]]
            if not last:
                acc[columns, 128 * SPANS[h][0] : 128 * SPANS[h][1]] = term
            else:
                for c in range(4):
                    for d in range(values):
                        spread[d, pl.ds(4 * m + c, 64, stride=16), :] = term[
                            64 * c : 64 * (c + 1), 128 * d : 128 * (d + 1)
                        ]
            return 0

        lax.fori_loop(0, 4, one_tile, 0, unroll=4 if last else 2)

    def term(h, group):
        if not h:
            c3[group].wait_recv()
        await_x(h, group)
        multiply(h, group)

    def round_off(h):
        start, stop = SPANS[h]

        def one_pair(pair, _):
            for d in range(start, stop):
                first = spread[d - start, pl.ds(pl.multiple_of(32 * pair, 16), 16), :]
                second = spread[d - start, pl.ds(pl.multiple_of(32 * pair + 16, 16), 16), :]
                at = slice(16 * d, 16 * (d + 1))
                ints[pair, at, 0:128] = jnp.where(low, first, pltpu.roll(second, 64, 1)).astype(BF16)
                ints[pair, at, 128:256] = jnp.where(low, pltpu.roll(first, 64, 1), second).astype(BF16)
            return 0

        lax.fori_loop(0, 32, one_pair, 0, unroll=8)

    c_across(0)

    def d_rows(half):
        rows[...] = d_raw[half].reshape(1280, 128).astype(F32)
        for h, (start, stop) in enumerate(SPANS):
            for d in range(start, stop):
                both = jnp.concatenate([rows[pl.ds(16 * odd + d, 40, stride=32), :] for odd in (0, 1)], axis=0)
                d_full[h][0, half, :, 128 * (d - start) : 128 * (d - start + 1)] = both.astype(BF16)

    own_d.wait()
    for half in (0, 1):
        for step_y in (1, 3, 2):
            dy[half, step_y].wait_recv()
        d_rows(half)
        own_start(0, half)
        x_start(0, 0, half)
        x_start(1, 0, half)
    own_start(1, 0)
    own_start(1, 1)
    for offset in OFFSETS[1:]:
        c_across(offset)
    c_forward(0)
    c_forward(1)
    step(0)
    c_forward(2)
    step(1)
    c_forward(3)
    c_forward(4)
    c_rows(0)
    step(2)
    step(3)
    c_rows(1)
    term(0, 0)
    step(4)
    term(1, 0)
    step(5)
    c_rows(2)
    term(0, 1)
    step(6)
    term(1, 1)
    step(7)
    step(8)
    c_rows(3)
    term(0, 2)
    step(9)
    c_rows(4)
    term(1, 2)
    step(10)
    step(11)
    step(12)
    term(0, 3)
    step(13)
    term(1, 3)
    amp_copy.wait_recv()
    term(0, 4)
    round_off(0)
    term(1, 4)
    round_off(1)

    finals = []
    for part in range(4):

        def one_pair(pair, _):
            total = jnp.dot(amps[...].reshape(256, 256), ints[pair], preferred_element_type=F32)
            columns = pl.ds(pl.multiple_of(128 * pair, 128), 128)
            for j in (0, 1):
                rounded = total[:, 128 * j : 128 * (j + 1)].astype(BF16)
                out_ref[2 * k + j, :, columns] = rounded[:128]
                result[j, :, columns] = rounded[128:]
            return 0

        lax.fori_loop(8 * part, 8 * (part + 1), one_pair, 0, unroll=8)
        columns = pl.ds(1024 * part, 1024)
        theirs = pltpu.make_async_remote_copy(
            src_ref=result.at[:, :, columns], dst_ref=out_ref.at[pl.ds(2 * k, 2), :, columns],
            send_sem=outs_send.at[part], recv_sem=outs_recv.at[part],
            device_id=device(x, y, z, k + 1), device_id_type=MESH,
        )
        theirs.start()
        finals.append(theirs)

    for copy in list(dy.values()) + list(c1.values()) + list(c1_other.values()) + list(cx.values()) + list(c2.values()) + list(c3.values()) + [amp_copy] + sent:
        copy.wait_send()
    for copy in finals:
        copy.wait()


def blocks_inward(in_ref, out_ref):
    columns = pl.ds(pl.multiple_of(1024 * pl.program_id(0), 1024), 1024)
    out_ref[...] = jnp.swapaxes(in_ref[:, :, columns], 0, 1)


def body(cholesky_c, cholesky_d, amplitudes):
    slab_c = jnp.transpose(cholesky_c, (0, 2, 1)).reshape(2, 20, 16, 1024)
    slab_d = jnp.transpose(cholesky_d, (0, 2, 1)).reshape(2, 20, 16, 1024)
    dma = pltpu.SemaphoreType.DMA
    out = pl.pallas_call(
        kernel,
        out_shape=pltpu.VMEM((4, 128, 4096), BF16),
        in_specs=[
            pl.BlockSpec(memory_space=pl.ANY),
            pl.BlockSpec(memory_space=pl.ANY),
            pl.BlockSpec(memory_space=pltpu.VMEM),
        ],
        out_specs=pl.BlockSpec(memory_space=pltpu.VMEM),
        scratch_shapes=[
            pltpu.VMEM((20, 16, 1024), BF16),
            pltpu.VMEM((2, 8, 10, 16, 128), BF16),
            pltpu.VMEM((8, 5, 16, 128), BF16),
            pltpu.VMEM((16, 4, 10, 16, 128), BF16),
            pltpu.VMEM((2, 4, 20, 16, 128), BF16),
            pltpu.VMEM((1280, 128), F32),
            pltpu.VMEM((16, 2, 80, 1024), BF16),
            *(pltpu.VMEM((16, 2, 80, 128 * (stop - start)), BF16) for start, stop in SPANS),
            pltpu.VMEM((1024, 2048), F32),
            pltpu.VMEM((SPANS[0][1], 1024, 128), F32),
            pltpu.VMEM((32, 256, 256), BF16),
            pltpu.VMEM((2, 128, 256), BF16),
            pltpu.VMEM((2, 128, 4096), BF16),
            dma((2,)), dma((2,)), dma((2, 8)), dma((2, 8)), dma((8, 2)), dma((8, 2)), dma((5, 3)), dma((5, 3)), dma((5,)), dma((5,)),
            dma((2, 3)), dma((2, 3)), dma((2, 14)), dma((2, 14)), dma((2, 2, 8)), dma((2, 2, 8)),
            dma((4,)), dma((4,)),
        ],
        compiler_params=pltpu.CompilerParams(
            collective_id=0, has_side_effects=True, vmem_limit_bytes=58 * 2**20
        ),
        cost_estimate=pl.CostEstimate(flops=13_000_000_000, bytes_accessed=8_000_000, transcendentals=0),
    )(slab_c, slab_d, amplitudes)
    return pl.pallas_call(
        blocks_inward,
        grid=(4,),
        out_shape=jax.ShapeDtypeStruct((128, 4, 4096), BF16),
        in_specs=[pl.BlockSpec(memory_space=pltpu.VMEM)],
        out_specs=pl.BlockSpec((128, 4, 1024), lambda i: (0, 0, i)),
        compiler_params=pltpu.CompilerParams(vmem_limit_bytes=24 * 2**20),
    )(out)


def solution(mesh):
    return jax.shard_map(
        body,
        mesh=mesh,
        in_specs=(P("vir", None, None), P("vir", None, None), P("occ", None)),
        out_specs=P("occ", "vir", None),
        check_vma=False,
    )
```

```python
import functools

import jax
import jax.numpy as jnp
from jax import lax
from jax.experimental import pallas as pl
from jax.experimental.pallas import tpu as pltpu
from jax.sharding import PartitionSpec as P

MESH = pl.DeviceIdType.MESH
F32 = jnp.float32
BF16 = jnp.bfloat16

NX, NY, NZ, NK = 4, 4, 8, 2
OFFSETS = (0, -1, 1, -2, 2, -3, 3, 4)
PARTS = ((0, 0), (0, 1), (1, 0), (1, 1))
ARRIVALS = tuple(
    tuple((sign * hops, h, half) for hops in (1, 2, 3) for h, half in PARTS) + ((4, 0, way), (4, 1, way))
    for way, sign in ((0, -1), (1, 1))
)
SPANS = ((0, 8), (8, 16))
GROUPS = ((0, 2), (2, 4), (6, 4), (10, 4), (14, 2))


def slot_of(offset, other):
    return 2 * OFFSETS.index(offset) + other


def place():
    v, o = lax.axis_index("vir"), lax.axis_index("occ")
    x = (o // NK) * 2 + v // (NZ * NY)
    return x, v % NY, (v // NY) % NZ, o % NK


def device(x, y, z, k):
    x, y, z, k = (x + NX) % NX, (y + NY) % NY, (z + NZ) % NZ, (k + NK) % NK
    return ((x % 2) * NZ + z) * NY + y, (x // 2) * NK + k


def kernel(
    c_ref, d_ref, amp_ref, out_ref,
    c_slab, c_send, c_in, c_raw, d_raw, rows, c_full, d_first, d_second, acc, spread, ints, amps, result,
    load_sem, amp_sems, c1_send, c1_recv, cx_send, cx_recv, c2_send, c2_recv, c3_send, c3_recv, dy_send, dy_recv,
    z_send, z_recv, x_send, x_recv, outs_send, outs_recv,
):
    x, y, z, k = place()
    x_low, share = x % 2, 5 * (x // 2)
    d_full = (d_first, d_second)
    low = lax.broadcasted_iota(jnp.int32, (16, 128), 1) < 64

    barrier = pltpu.get_barrier_semaphore()
    greeted = []
    greeted += [device(x, y, z + offset, k) for offset in OFFSETS if offset]
    greeted += [device(x + step, y, z, k) for step in (1, 3)]
    greeted += [device(x, y + step, z, k) for step in (1, 2, 3)]
    greeted.append(device(x, y, z, k + 1))
    for target in greeted:
        pl.semaphore_signal(barrier, inc=1, device_id=target, device_id_type=MESH)

    load = pltpu.make_async_copy(c_ref.at[k], c_slab, load_sem.at[0])
    load.start()
    own_d = pltpu.make_async_copy(
        d_ref.at[:, :, :, pl.ds(pl.multiple_of(256 * y + 128 * k, 128), 128)], d_raw.at[:, y], load_sem.at[1]
    )
    own_d.start()
    pl.semaphore_wait(barrier, len(greeted))

    def columns_of(to, half):
        return d_ref.at[half, :, :, pl.ds(pl.multiple_of(256 * to + 128 * k, 128), 128)]

    dy = {}
    for half in (0, 1):
        for step in (1, 3, 2):
            to = (y + step) % NY
            copy = pltpu.make_async_remote_copy(
                src_ref=columns_of(to, half), dst_ref=d_raw.at[half, y],
                send_sem=dy_send.at[half, step - 1], recv_sem=dy_recv.at[half, step - 1],
                device_id=device(x, to, z, k), device_id_type=MESH,
            )
            copy.start()
            dy[half, step] = copy
    load.wait()

    def pair_up(p, _):
        for m in range(8):
            first = c_slab[2 * p, :, 128 * m : 128 * (m + 1)].astype(F32)
            second = c_slab[2 * p + 1, :, 128 * m : 128 * (m + 1)].astype(F32)
            c_send[m // 4, 2 * m % 8, p] = jnp.where(low, first, pltpu.roll(second, 64, 1)).astype(BF16)
            c_send[m // 4, 2 * m % 8 + 1, p] = jnp.where(low, pltpu.roll(first, 64, 1), second).astype(BF16)
        return 0

    lax.fori_loop(0, 10, pair_up, 0)
    c1, c1_other = {}, {}
    for offset in OFFSETS[1:]:
        to_z = (z - offset + NZ) % NZ
        index = OFFSETS.index(offset)
        for other, copies in ((1, c1_other), (0, c1)):
            copies[offset] = pltpu.make_async_remote_copy(
                src_ref=c_send.at[1 - x_low, to_z, pl.ds(share, 5)] if other else c_send.at[x_low, to_z],
                dst_ref=c_in.at[index] if other else c_raw.at[slot_of(offset, 0), y],
                send_sem=c1_send.at[other, index], recv_sem=c1_recv.at[other, index],
                device_id=device(x, y, to_z, k), device_id_type=MESH,
            )
            copies[offset].start()
    own_c = pltpu.make_async_copy(c_send.at[x_low, z], c_raw.at[0, y], load_sem.at[0])
    own_c.start()

    old, new = (lax.broadcasted_iota(jnp.int32, (256, 256), axis) for axis in (0, 1))
    swap = (old == (new % 16) * 16 + new // 16).astype(F32).astype(BF16)
    amps[0] = jnp.dot(amp_ref[...], swap, preferred_element_type=F32).astype(BF16)
    amp_copy = pltpu.make_async_remote_copy(
        src_ref=amps.at[0], dst_ref=amps.at[1], send_sem=amp_sems.at[0], recv_sem=amp_sems.at[1],
        device_id=device(x, y, z, k + 1), device_id_type=MESH,
    )
    amp_copy.start()

    cx = {}

    def c_across(offset):
        index = OFFSETS.index(offset)
        if offset:
            c1_other[offset].wait_recv()
        for step in (1, 3):
            cx[offset, step] = pltpu.make_async_remote_copy(
                src_ref=c_in.at[index] if offset else c_send.at[1 - x_low, z, pl.ds(share, 5)],
                dst_ref=c_raw.at[slot_of(offset, 1), y, pl.ds(share, 5)],
                send_sem=cx_send.at[index, step // 2], recv_sem=cx_recv.at[index, step // 2],
                device_id=device(x + step, y, z, k), device_id_type=MESH,
            )
            cx[offset, step].start()

    c2 = {}

    def c_forward(group):
        start, count = GROUPS[group]
        for offset in OFFSETS[start // 2 : (start + count) // 2]:
            if offset:
                c1[offset].wait_recv()
            else:
                own_c.wait()
            for step in (1, 3):
                cx[offset, step].wait_recv()
        mine = c_raw.at[pl.ds(start, count), y]
        for step in (1, 3, 2):
            copy = pltpu.make_async_remote_copy(
                src_ref=mine, dst_ref=mine,
                send_sem=c2_send.at[group, step - 1], recv_sem=c2_recv.at[group, step - 1],
                device_id=device(x, y + step, z, k), device_id_type=MESH,
            )
            copy.start()
            c2[group, step] = copy

    c3 = {}

    def c_rows(group):
        start, count = GROUPS[group]
        for step in (1, 2, 3):
            c2[group, step].wait_recv()

        def one_slot(slot, _):
            rows[0:640, :] = c_raw[slot].reshape(640, 128).astype(F32)
            lower = lax.broadcasted_iota(jnp.int32, (40, 128), 1) < 64
            for m in range(8):
                first = rows[pl.ds(2 * m, 40, stride=16), :]
                second = rows[pl.ds(2 * m + 1, 40, stride=16), :]
                both = jnp.concatenate(
                    [
                        jnp.where(lower, first, pltpu.roll(second, 64, 1)),
                        jnp.where(lower, pltpu.roll(first, 64, 1), second),
                    ],
                    axis=0,
                )
                c_full[slot, k, :, 128 * m : 128 * (m + 1)] = both.astype(BF16)
            return 0

        lax.fori_loop(start, start + count, one_slot, 0)
        half = c_full.at[pl.ds(start, count), k]
        c3[group] = pltpu.make_async_remote_copy(
            src_ref=half, dst_ref=half, send_sem=c3_send.at[group], recv_sem=c3_recv.at[group],
            device_id=device(x, y, z, k + 1), device_id_type=MESH,
        )
        c3[group].start()

    sent = []

    def x_copy(h, offset, half):
        copy = pltpu.make_async_remote_copy(
            src_ref=d_full[h].at[slot_of(offset, 0), half],
            dst_ref=d_full[h].at[slot_of(offset, 1), half],
            send_sem=x_send.at[h, half, OFFSETS.index(offset)],
            recv_sem=x_recv.at[h, half, OFFSETS.index(offset)],
            device_id=device(x + 1 - 2 * (half if offset else h), y, z, k), device_id_type=MESH,
        )
        return copy

    def x_start(h, offset, half):
        copy = x_copy(h, offset, half)
        copy.start()
        sent.append(copy)

    def z_copy(way, i):
        offset, h, half = ARRIVALS[way][i]
        before = (offset + 1 if way == 0 else offset - 1) if offset != 4 else (-3 if way == 0 else 3)
        return pltpu.make_async_remote_copy(
            src_ref=d_full[h].at[slot_of(before, 0), half],
            dst_ref=d_full[h].at[slot_of(offset, 0), half],
            send_sem=z_send.at[way, i], recv_sem=z_recv.at[way, i],
            device_id=device(x, y, z + 1 - 2 * way, k), device_id_type=MESH,
        )

    def z_start(way, i):
        copy = z_copy(way, i)
        copy.start()
        sent.append(copy)

    def own_start(h, half):
        for way in (0, 1):
            z_start(way, PARTS.index((h, half)))

    def step(i):
        for way in (0, 1):
            z_copy(way, i).wait_recv()
            offset, h, half = ARRIVALS[way][i]
            after = offset - 1 if way == 0 else offset + 1
            onward = (4 if after == -4 else after, h, half)
            if onward in ARRIVALS[way]:
                z_start(way, ARRIVALS[way].index(onward))
            x_start(h, offset, half)

    def await_x(h, group):
        start, count = GROUPS[group]
        for slot in range(start, start + count, 2):
            for half in (0, 1):
                x_copy(h, OFFSETS[slot // 2], half).wait_recv()

    def multiply(h, group):
        start, count = GROUPS[group]
        last = group == len(GROUPS) - 1
        values = SPANS[h][1] - SPANS[h][0]

        def one_tile(m, _):
            columns = pl.ds(pl.multiple_of(256 * m, 256), 256)
            left = c_full[start : start + count, :, :, columns].reshape(160 * count, 256)
            right = d_full[h][start : start + count].reshape(160 * count, 128 * values)
            term = lax.dot_general(left, right, (((0,), (0,)), ((), ())), preferred_element_type=F32)
            if group:
                term += acc[columns, 128 * SPANS[h][0] : 128 * SPANS[h][1]]
            if not last:
                acc[columns, 128 * SPANS[h][0] : 128 * SPANS[h][1]] = term
            else:
                for c in range(4):
                    for d in range(values):
                        spread[d, pl.ds(4 * m + c, 64, stride=16), :] = term[
                            64 * c : 64 * (c + 1), 128 * d : 128 * (d + 1)
                        ]
            return 0

        lax.fori_loop(0, 4, one_tile, 0, unroll=4)

    def term(h, group):
        if not h:
            c3[group].wait_recv()
        await_x(h, group)
        multiply(h, group)

    def round_off(h):
        start, stop = SPANS[h]

        def one_pair(pair, _):
            for d in range(start, stop):
                first = spread[d - start, pl.ds(pl.multiple_of(32 * pair, 16), 16), :]
                second = spread[d - start, pl.ds(pl.multiple_of(32 * pair + 16, 16), 16), :]
                at = slice(16 * d, 16 * (d + 1))
                ints[pair, at, 0:128] = jnp.where(low, first, pltpu.roll(second, 64, 1)).astype(BF16)
                ints[pair, at, 128:256] = jnp.where(low, pltpu.roll(first, 64, 1), second).astype(BF16)
            return 0

        lax.fori_loop(0, 32, one_pair, 0, unroll=8)

    c_across(0)

    def d_rows(half):
        rows[...] = d_raw[half].reshape(1280, 128).astype(F32)
        for h, (start, stop) in enumerate(SPANS):
            for d in range(start, stop):
                both = jnp.concatenate([rows[pl.ds(16 * odd + d, 40, stride=32), :] for odd in (0, 1)], axis=0)
                d_full[h][0, half, :, 128 * (d - start) : 128 * (d - start + 1)] = both.astype(BF16)

    own_d.wait()
    for half in (0, 1):
        for step_y in (1, 3, 2):
            dy[half, step_y].wait_recv()
        d_rows(half)
        own_start(0, half)
        x_start(0, 0, half)
        x_start(1, 0, half)
    own_start(1, 0)
    own_start(1, 1)
    for offset in OFFSETS[1:]:
        c_across(offset)
    c_forward(0)
    c_forward(1)
    step(0)
    c_forward(2)
    step(1)
    c_forward(3)
    c_forward(4)
    c_rows(0)
    step(2)
    step(3)
    c_rows(1)
    term(0, 0)
    step(4)
    term(1, 0)
    step(5)
    c_rows(2)
    term(0, 1)
    step(6)
    term(1, 1)
    step(7)
    step(8)
    c_rows(3)
    term(0, 2)
    step(9)
    c_rows(4)
    term(1, 2)
    step(10)
    for copy in [*dy.values(), *c1.values(), *c1_other.values(), *cx.values(), *c2.values(), *c3.values()]:
        copy.wait_send()
    step(11)
    step(12)
    term(0, 3)
    step(13)
    term(1, 3)
    settled = sent[:40]
    for copy in settled:
        copy.wait_send()
    amp_copy.wait_recv()
    term(0, 4)
    round_off(0)
    term(1, 4)
    round_off(1)

    finals = []
    for part in range(4):

        def one_pair(pair, _):
            total = jnp.dot(amps[...].reshape(256, 256), ints[pair], preferred_element_type=F32)
            columns = pl.ds(pl.multiple_of(128 * pair, 128), 128)
            for j in (0, 1):
                rounded = total[:, 128 * j : 128 * (j + 1)].astype(BF16)
                out_ref[2 * k + j, :, columns] = rounded[:128]
                result[j, :, columns] = rounded[128:]
            return 0

        lax.fori_loop(8 * part, 8 * (part + 1), one_pair, 0, unroll=8)
        columns = pl.ds(1024 * part, 1024)
        theirs = pltpu.make_async_remote_copy(
            src_ref=result.at[:, :, columns], dst_ref=out_ref.at[pl.ds(2 * k, 2), :, columns],
            send_sem=outs_send.at[part], recv_sem=outs_recv.at[part],
            device_id=device(x, y, z, k + 1), device_id_type=MESH,
        )
        theirs.start()
        finals.append(theirs)

    for copy in [amp_copy] + sent[len(settled) :]:
        copy.wait_send()
    for copy in finals:
        copy.wait()


def blocks_inward(in_ref, out_ref):
    columns = pl.ds(pl.multiple_of(1024 * pl.program_id(0), 1024), 1024)
    out_ref[...] = jnp.swapaxes(in_ref[:, :, columns], 0, 1)


def body(cholesky_c, cholesky_d, amplitudes):
    slab_c = jnp.transpose(cholesky_c, (0, 2, 1)).reshape(2, 20, 16, 1024)
    slab_d = jnp.transpose(cholesky_d, (0, 2, 1)).reshape(2, 20, 16, 1024)
    dma = pltpu.SemaphoreType.DMA
    out = pl.pallas_call(
        kernel,
        out_shape=pltpu.VMEM((4, 128, 4096), BF16),
        in_specs=[
            pl.BlockSpec(memory_space=pl.ANY),
            pl.BlockSpec(memory_space=pl.ANY),
            pl.BlockSpec(memory_space=pltpu.VMEM),
        ],
        out_specs=pl.BlockSpec(memory_space=pltpu.VMEM),
        scratch_shapes=[
            pltpu.VMEM((20, 16, 1024), BF16),
            pltpu.VMEM((2, 8, 10, 16, 128), BF16),
            pltpu.VMEM((8, 5, 16, 128), BF16),
            pltpu.VMEM((16, 4, 10, 16, 128), BF16),
            pltpu.VMEM((2, 4, 20, 16, 128), BF16),
            pltpu.VMEM((1280, 128), F32),
            pltpu.VMEM((16, 2, 80, 1024), BF16),
            *(pltpu.VMEM((16, 2, 80, 128 * (stop - start)), BF16) for start, stop in SPANS),
            pltpu.VMEM((1024, 2048), F32),
            pltpu.VMEM((SPANS[0][1], 1024, 128), F32),
            pltpu.VMEM((32, 256, 256), BF16),
            pltpu.VMEM((2, 128, 256), BF16),
            pltpu.VMEM((2, 128, 4096), BF16),
            dma((2,)), dma((2,)), dma((2, 8)), dma((2, 8)), dma((8, 2)), dma((8, 2)), dma((5, 3)), dma((5, 3)), dma((5,)), dma((5,)),
            dma((2, 3)), dma((2, 3)), dma((2, 14)), dma((2, 14)), dma((2, 2, 8)), dma((2, 2, 8)),
            dma((4,)), dma((4,)),
        ],
        compiler_params=pltpu.CompilerParams(
            collective_id=0, has_side_effects=True, vmem_limit_bytes=59 * 2**20
        ),
        cost_estimate=pl.CostEstimate(flops=13_000_000_000, bytes_accessed=8_000_000, transcendentals=0),
    )(slab_c, slab_d, amplitudes)
    return pl.pallas_call(
        blocks_inward,
        grid=(4,),
        out_shape=jax.ShapeDtypeStruct((128, 4, 4096), BF16),
        in_specs=[pl.BlockSpec(memory_space=pltpu.VMEM)],
        out_specs=pl.BlockSpec((128, 4, 1024), lambda i: (0, 0, i)),
        compiler_params=pltpu.CompilerParams(vmem_limit_bytes=24 * 2**20),
    )(out)


def solution(mesh):
    return jax.shard_map(
        body,
        mesh=mesh,
        in_specs=(P("vir", None, None), P("vir", None, None), P("occ", None)),
        out_specs=P("occ", "vir", None),
        check_vma=False,
    )
```

```python
import functools

import jax
import jax.numpy as jnp
from jax import lax
from jax.experimental import pallas as pl
from jax.experimental.pallas import tpu as pltpu
from jax.sharding import PartitionSpec as P

MESH = pl.DeviceIdType.MESH
F32 = jnp.float32
BF16 = jnp.bfloat16

NX, NY, NZ, NK = 4, 4, 8, 2
OFFSETS = (0, -1, 1, -2, 2, -3, 3, 4)
PARTS = ((0, 0), (0, 1), (1, 0), (1, 1))
ARRIVALS = tuple(
    tuple((sign * hops, h, half) for hops in (1, 2, 3) for h, half in PARTS) + ((4, 0, way), (4, 1, way))
    for way, sign in ((0, -1), (1, 1))
)
SPANS = ((0, 8), (8, 16))
GROUPS = ((0, 2), (2, 4), (6, 4), (10, 4), (14, 2))


def slot_of(offset, other):
    return 2 * OFFSETS.index(offset) + other


def place():
    v, o = lax.axis_index("vir"), lax.axis_index("occ")
    x = (o // NK) * 2 + v // (NZ * NY)
    return x, v % NY, (v // NY) % NZ, o % NK


def device(x, y, z, k):
    x, y, z, k = (x + NX) % NX, (y + NY) % NY, (z + NZ) % NZ, (k + NK) % NK
    return ((x % 2) * NZ + z) * NY + y, (x // 2) * NK + k


def kernel(
    c_ref, d_ref, amp_ref, out_ref,
    c_slab, c_send, c_in, c_raw, d_raw, rows, c_full, d_first, d_second, acc, spread, ints, amps, result,
    load_sem, amp_sems, c1_send, c1_recv, cx_send, cx_recv, c2_send, c2_recv, c3_send, c3_recv, dy_send, dy_recv,
    z_send, z_recv, x_send, x_recv, outs_send, outs_recv,
):
    x, y, z, k = place()
    x_low, share = x % 2, 5 * (x // 2)
    d_full = (d_first, d_second)
    low = lax.broadcasted_iota(jnp.int32, (16, 128), 1) < 64

    barrier = pltpu.get_barrier_semaphore()
    greeted = []
    greeted += [device(x, y, z + offset, k) for offset in OFFSETS if offset]
    greeted += [device(x + step, y, z, k) for step in (1, 3)]
    greeted += [device(x, y + step, z, k) for step in (1, 2, 3)]
    greeted.append(device(x, y, z, k + 1))
    for target in greeted:
        pl.semaphore_signal(barrier, inc=1, device_id=target, device_id_type=MESH)

    load = pltpu.make_async_copy(c_ref.at[k], c_slab, load_sem.at[0])
    load.start()
    own_d = pltpu.make_async_copy(
        d_ref.at[:, :, :, pl.ds(pl.multiple_of(256 * y + 128 * k, 128), 128)], d_raw.at[:, y], load_sem.at[1]
    )
    own_d.start()
    pl.semaphore_wait(barrier, len(greeted))

    def columns_of(to, half):
        return d_ref.at[half, :, :, pl.ds(pl.multiple_of(256 * to + 128 * k, 128), 128)]

    dy = {}
    for half in (0, 1):
        for step in (1, 3, 2):
            to = (y + step) % NY
            copy = pltpu.make_async_remote_copy(
                src_ref=columns_of(to, half), dst_ref=d_raw.at[half, y],
                send_sem=dy_send.at[half, step - 1], recv_sem=dy_recv.at[half, step - 1],
                device_id=device(x, to, z, k), device_id_type=MESH,
            )
            copy.start()
            dy[half, step] = copy
    load.wait()

    def pair_up(p, _):
        for m in range(8):
            first = c_slab[2 * p, :, 128 * m : 128 * (m + 1)].astype(F32)
            second = c_slab[2 * p + 1, :, 128 * m : 128 * (m + 1)].astype(F32)
            c_send[m // 4, 2 * m % 8, p] = jnp.where(low, first, pltpu.roll(second, 64, 1)).astype(BF16)
            c_send[m // 4, 2 * m % 8 + 1, p] = jnp.where(low, pltpu.roll(first, 64, 1), second).astype(BF16)
        return 0

    lax.fori_loop(0, 10, pair_up, 0)
    c1, c1_other = {}, {}
    for offset in OFFSETS[1:]:
        to_z = (z - offset + NZ) % NZ
        index = OFFSETS.index(offset)
        for other, copies in ((1, c1_other), (0, c1)):
            copies[offset] = pltpu.make_async_remote_copy(
                src_ref=c_send.at[1 - x_low, to_z, pl.ds(share, 5)] if other else c_send.at[x_low, to_z],
                dst_ref=c_in.at[index] if other else c_raw.at[slot_of(offset, 0), y],
                send_sem=c1_send.at[other, index], recv_sem=c1_recv.at[other, index],
                device_id=device(x, y, to_z, k), device_id_type=MESH,
            )
            copies[offset].start()
    own_c = pltpu.make_async_copy(c_send.at[x_low, z], c_raw.at[0, y], load_sem.at[0])
    own_c.start()

    old, new = (lax.broadcasted_iota(jnp.int32, (256, 256), axis) for axis in (0, 1))
    swap = (old == (new % 16) * 16 + new // 16).astype(F32).astype(BF16)
    amps[0] = jnp.dot(amp_ref[...], swap, preferred_element_type=F32).astype(BF16)
    amp_copy = pltpu.make_async_remote_copy(
        src_ref=amps.at[0], dst_ref=amps.at[1], send_sem=amp_sems.at[0], recv_sem=amp_sems.at[1],
        device_id=device(x, y, z, k + 1), device_id_type=MESH,
    )
    amp_copy.start()

    cx = {}

    def c_across(offset):
        index = OFFSETS.index(offset)
        if offset:
            c1_other[offset].wait_recv()
        for step in (1, 3):
            cx[offset, step] = pltpu.make_async_remote_copy(
                src_ref=c_in.at[index] if offset else c_send.at[1 - x_low, z, pl.ds(share, 5)],
                dst_ref=c_raw.at[slot_of(offset, 1), y, pl.ds(share, 5)],
                send_sem=cx_send.at[index, step // 2], recv_sem=cx_recv.at[index, step // 2],
                device_id=device(x + step, y, z, k), device_id_type=MESH,
            )
            cx[offset, step].start()

    c2 = {}

    def c_forward(group):
        start, count = GROUPS[group]
        for offset in OFFSETS[start // 2 : (start + count) // 2]:
            if offset:
                c1[offset].wait_recv()
            else:
                own_c.wait()
            for step in (1, 3):
                cx[offset, step].wait_recv()
        mine = c_raw.at[pl.ds(start, count), y]
        for step in (1, 3, 2):
            copy = pltpu.make_async_remote_copy(
                src_ref=mine, dst_ref=mine,
                send_sem=c2_send.at[group, step - 1], recv_sem=c2_recv.at[group, step - 1],
                device_id=device(x, y + step, z, k), device_id_type=MESH,
            )
            copy.start()
            c2[group, step] = copy

    c3 = {}

    def c_rows(group):
        start, count = GROUPS[group]
        for step in (1, 2, 3):
            c2[group, step].wait_recv()

        def one_slot(slot, _):
            rows[0:640, :] = c_raw[slot].reshape(640, 128).astype(F32)
            lower = lax.broadcasted_iota(jnp.int32, (40, 128), 1) < 64
            for m in range(8):
                first = rows[pl.ds(2 * m, 40, stride=16), :]
                second = rows[pl.ds(2 * m + 1, 40, stride=16), :]
                both = jnp.concatenate(
                    [
                        jnp.where(lower, first, pltpu.roll(second, 64, 1)),
                        jnp.where(lower, pltpu.roll(first, 64, 1), second),
                    ],
                    axis=0,
                )
                c_full[slot, k, :, 128 * m : 128 * (m + 1)] = both.astype(BF16)
            return 0

        lax.fori_loop(start, start + count, one_slot, 0)
        half = c_full.at[pl.ds(start, count), k]
        c3[group] = pltpu.make_async_remote_copy(
            src_ref=half, dst_ref=half, send_sem=c3_send.at[group], recv_sem=c3_recv.at[group],
            device_id=device(x, y, z, k + 1), device_id_type=MESH,
        )
        c3[group].start()

    sent = []

    def x_copy(h, offset, half):
        copy = pltpu.make_async_remote_copy(
            src_ref=d_full[h].at[slot_of(offset, 0), half],
            dst_ref=d_full[h].at[slot_of(offset, 1), half],
            send_sem=x_send.at[h, half, OFFSETS.index(offset)],
            recv_sem=x_recv.at[h, half, OFFSETS.index(offset)],
            device_id=device(x + 1 - 2 * (half if offset else h), y, z, k), device_id_type=MESH,
        )
        return copy

    def x_start(h, offset, half):
        copy = x_copy(h, offset, half)
        copy.start()
        sent.append(copy)

    def z_copy(way, i):
        offset, h, half = ARRIVALS[way][i]
        before = (offset + 1 if way == 0 else offset - 1) if offset != 4 else (-3 if way == 0 else 3)
        return pltpu.make_async_remote_copy(
            src_ref=d_full[h].at[slot_of(before, 0), half],
            dst_ref=d_full[h].at[slot_of(offset, 0), half],
            send_sem=z_send.at[way, i], recv_sem=z_recv.at[way, i],
            device_id=device(x, y, z + 1 - 2 * way, k), device_id_type=MESH,
        )

    def z_start(way, i):
        copy = z_copy(way, i)
        copy.start()
        sent.append(copy)

    def own_start(h, half):
        for way in (0, 1):
            z_start(way, PARTS.index((h, half)))

    def step(i):
        for way in (0, 1):
            z_copy(way, i).wait_recv()
            offset, h, half = ARRIVALS[way][i]
            after = offset - 1 if way == 0 else offset + 1
            onward = (4 if after == -4 else after, h, half)
            if onward in ARRIVALS[way]:
                z_start(way, ARRIVALS[way].index(onward))
            x_start(h, offset, half)

    def await_x(h, group):
        start, count = GROUPS[group]
        for slot in range(start, start + count, 2):
            for half in (0, 1):
                x_copy(h, OFFSETS[slot // 2], half).wait_recv()

    def multiply(h, group):
        start, count = GROUPS[group]
        last = group == len(GROUPS) - 1
        values = SPANS[h][1] - SPANS[h][0]

        def one_tile(m, _):
            columns = pl.ds(pl.multiple_of(256 * m, 256), 256)
            left = c_full[start : start + count, :, :, columns].reshape(160 * count, 256)
            right = d_full[h][start : start + count].reshape(160 * count, 128 * values)
            term = lax.dot_general(left, right, (((0,), (0,)), ((), ())), preferred_element_type=F32)
            if group:
                term += acc[columns, 128 * SPANS[h][0] : 128 * SPANS[h][1]]
            if not last:
                acc[columns, 128 * SPANS[h][0] : 128 * SPANS[h][1]] = term
            else:
                for c in range(4):
                    for d in range(values):
                        spread[d, pl.ds(4 * m + c, 64, stride=16), :] = term[
                            64 * c : 64 * (c + 1), 128 * d : 128 * (d + 1)
                        ]
            return 0

        lax.fori_loop(0, 4, one_tile, 0, unroll=4 if last else 2)

    def term(h, group):
        if not h:
            c3[group].wait_recv()
        await_x(h, group)
        multiply(h, group)

    def round_off(h):
        start, stop = SPANS[h]

        def one_pair(pair, _):
            for d in range(start, stop):
                first = spread[d - start, pl.ds(pl.multiple_of(32 * pair, 16), 16), :]
                second = spread[d - start, pl.ds(pl.multiple_of(32 * pair + 16, 16), 16), :]
                at = slice(16 * d, 16 * (d + 1))
                ints[pair, at, 0:128] = jnp.where(low, first, pltpu.roll(second, 64, 1)).astype(BF16)
                ints[pair, at, 128:256] = jnp.where(low, pltpu.roll(first, 64, 1), second).astype(BF16)
            return 0

        lax.fori_loop(0, 32, one_pair, 0, unroll=8)

    c_across(0)

    def d_rows(half):
        rows[0:1280, :] = d_raw[half].reshape(1280, 128).astype(F32)
        for h, (start, stop) in enumerate(SPANS):
            for d in range(start, stop):
                both = jnp.concatenate([rows[pl.ds(16 * odd + d, 40, stride=32), :] for odd in (0, 1)], axis=0)
                d_full[h][0, half, :, 128 * (d - start) : 128 * (d - start + 1)] = both.astype(BF16)

    own_d.wait()
    for half in (0, 1):
        for step_y in (1, 3, 2):
            dy[half, step_y].wait_recv()
        d_rows(half)
        own_start(0, half)
        x_start(0, 0, half)
        x_start(1, 0, half)
    own_start(1, 0)
    own_start(1, 1)
    for offset in OFFSETS[1:]:
        c_across(offset)
    c_forward(0)
    c_forward(1)
    step(0)
    c_forward(2)
    step(1)
    c_forward(3)
    c_forward(4)
    c_rows(0)
    step(2)
    step(3)
    c_rows(1)
    term(0, 0)
    step(4)
    term(1, 0)
    step(5)
    c_rows(2)
    term(0, 1)
    step(6)
    term(1, 1)
    step(7)
    step(8)
    c_rows(3)
    term(0, 2)
    step(9)
    c_rows(4)
    term(1, 2)
    step(10)
    step(11)
    step(12)
    term(0, 3)
    step(13)
    term(1, 3)
    amp_copy.wait_recv()
    term(0, 4)
    round_off(0)
    term(1, 4)
    round_off(1)

    finals = []
    for part in range(4):

        def one_pair(pair, _):
            total = jnp.dot(amps[...].reshape(256, 256), ints[pair], preferred_element_type=F32)
            columns = pl.ds(pl.multiple_of(128 * pair, 128), 128)
            for j in (0, 1):
                rounded = total[:, 128 * j : 128 * (j + 1)].astype(BF16)
                out_ref[2 * k + j, :, columns] = rounded[:128]
                result[j, :, columns] = rounded[128:]
            return 0

        lax.fori_loop(8 * part, 8 * (part + 1), one_pair, 0, unroll=8)
        columns = pl.ds(1024 * part, 1024)
        theirs = pltpu.make_async_remote_copy(
            src_ref=result.at[:, :, columns], dst_ref=out_ref.at[pl.ds(2 * k, 2), :, columns],
            send_sem=outs_send.at[part], recv_sem=outs_recv.at[part],
            device_id=device(x, y, z, k + 1), device_id_type=MESH,
        )
        theirs.start()
        finals.append(theirs)

    for copy in list(dy.values()) + list(c1.values()) + list(c1_other.values()) + list(cx.values()) + list(c2.values()) + list(c3.values()) + [amp_copy] + sent:
        copy.wait_send()
    for copy in finals:
        copy.wait()


def blocks_inward(in_ref, out_ref):
    columns = pl.ds(pl.multiple_of(1024 * pl.program_id(0), 1024), 1024)
    out_ref[...] = jnp.swapaxes(in_ref[:, :, columns], 0, 1)


def body(cholesky_c, cholesky_d, amplitudes):
    slab_c = jnp.transpose(cholesky_c, (0, 2, 1)).reshape(2, 20, 16, 1024)
    slab_d = jnp.transpose(cholesky_d, (0, 2, 1)).reshape(2, 20, 16, 1024)
    dma = pltpu.SemaphoreType.DMA
    out = pl.pallas_call(
        kernel,
        out_shape=pltpu.VMEM((4, 128, 4096), BF16),
        in_specs=[
            pl.BlockSpec(memory_space=pl.ANY),
            pl.BlockSpec(memory_space=pl.ANY),
            pl.BlockSpec(memory_space=pltpu.VMEM),
        ],
        out_specs=pl.BlockSpec(memory_space=pltpu.VMEM),
        scratch_shapes=[
            pltpu.VMEM((20, 16, 1024), BF16),
            pltpu.VMEM((2, 8, 10, 16, 128), BF16),
            pltpu.VMEM((8, 5, 16, 128), BF16),
            pltpu.VMEM((16, 4, 10, 16, 128), BF16),
            pltpu.VMEM((2, 4, 20, 16, 128), BF16),
            pltpu.VMEM((1312, 128), F32),
            pltpu.VMEM((16, 2, 80, 1024), BF16),
            *(pltpu.VMEM((16, 2, 80, 128 * (stop - start)), BF16) for start, stop in SPANS),
            pltpu.VMEM((1024, 2048), F32),
            pltpu.VMEM((SPANS[0][1], 1040, 128), F32),
            pltpu.VMEM((32, 256, 256), BF16),
            pltpu.VMEM((2, 128, 256), BF16),
            pltpu.VMEM((2, 128, 4096), BF16),
            dma((2,)), dma((2,)), dma((2, 8)), dma((2, 8)), dma((8, 2)), dma((8, 2)), dma((5, 3)), dma((5, 3)), dma((5,)), dma((5,)),
            dma((2, 3)), dma((2, 3)), dma((2, 14)), dma((2, 14)), dma((2, 2, 8)), dma((2, 2, 8)),
            dma((4,)), dma((4,)),
        ],
        compiler_params=pltpu.CompilerParams(
            collective_id=0, has_side_effects=True, vmem_limit_bytes=58 * 2**20
        ),
        cost_estimate=pl.CostEstimate(flops=13_000_000_000, bytes_accessed=8_000_000, transcendentals=0),
    )(slab_c, slab_d, amplitudes)
    return pl.pallas_call(
        blocks_inward,
        grid=(4,),
        out_shape=jax.ShapeDtypeStruct((128, 4, 4096), BF16),
        in_specs=[pl.BlockSpec(memory_space=pltpu.VMEM)],
        out_specs=pl.BlockSpec((128, 4, 1024), lambda i: (0, 0, i)),
        compiler_params=pltpu.CompilerParams(vmem_limit_bytes=24 * 2**20),
    )(out)


def solution(mesh):
    return jax.shard_map(
        body,
        mesh=mesh,
        in_specs=(P("vir", None, None), P("vir", None, None), P("occ", None)),
        out_specs=P("occ", "vir", None),
        check_vma=False,
    )
```
